32 devices in a mesh: groups: 2 (over y), dp: 8 (over z, x), tensor: 2 (over core).
Axes of the slice: x: 2, y: 2, z: 4, core: 2. Of those that a mesh axis runs over, the one named last changes fastest.
Arguments:
- queries: bfloat16 [2048, 8192], P(('groups', 'dp'), 'tensor'), parts along dimension 0, may hold values from -14 to 14
- answer_prompt: int32 [2048, 1], P(('groups', 'dp')), parts along dimension 0, may hold values from 0 to 7; in each aligned block of 128 rows (0 to 127, 128 to 255, ...) at most 32 rows name the same one
- prompt_owner: int32 [16], P('groups'), parts along dimension 0, may hold values from 0 to 7, each once
- context_keys: bfloat16 [16384, 1024], P(('groups', 'dp'), 'tensor'), parts along dimension 0, may hold values from -8 to 8
- context_values: bfloat16 [16384, 1024], P(('groups', 'dp'), 'tensor'), parts along dimension 0, may hold values from -6 to 6
- score_weight: float32 [8192], P('tensor'), may hold values from -6 to 6
Outputs:
- token_score: float32 [2048], P(('groups', 'dp')), parts along dimension 0
The draws below stay inside these ranges and needn't reach their ends.
There are 2 independent parts, one for each index of `groups`. The reference program is written for one: setup_inputs(seed, part) draws one part's arguments, and reference() takes and returns one part's arrays. A program takes and returns all parts, laid end to end along the dimension named above; an argument that names none is the same for every part. Nothing has to cross between parts.
Inputs may be any that keep to these rules, and one draw needn't show every extreme that they name: `answer_prompt`: among the 128 answer tokens of one replica at most 32 name the same prompt, and 32 is reached; every prompt is named by some token. `prompt_owner`: each replica holds exactly one prompt's context.
All inputs are finite; a program needn't handle non-finite values.
Results may differ from the reference program's by a relative error of at most 0.0042.
Values may be sent and summed in bfloat16 or wider, within the bound.
No kernel may reach another device: no remote copies, remote signals or barrier semaphores. Data moves between devices by JAX's collectives and lax.ppermute only.
A program may use at most 64 MiB of HBM per device.

```python
import math
import jax
import jax.numpy as jnp
import numpy as np
from jax import lax

HEADS = 64
KV_HEADS = 8
HD = 128
TOK_DEV = 128
CTX = 1024
TOKENS = 1024
CAP = 32
N_DP = 8


def draw_queries(key, part):
    key = jax.random.fold_in(key, 11)
    values_drawn = jnp.clip(jax.random.normal(key, (TOKENS, HEADS, HD), jnp.float32), -6.0, 6.0)
    return values_drawn.reshape(TOKENS, HEADS * HD).astype(jnp.bfloat16)


def draw_context_keys(key, part):
    key = jax.random.fold_in(key, 23)
    values_drawn = jnp.clip(jax.random.normal(key, (N_DP * CTX, KV_HEADS, HD), jnp.float32), -6.0, 6.0)
    return values_drawn.reshape(N_DP * CTX, KV_HEADS * HD).astype(jnp.bfloat16)


def block_levels(key, dims, split, smallest, top_value):
    gain, own = 1.0, jax.random.fold_in(key, 6)
    for dim, blocks in split:
        steps = jnp.exp(jax.random.uniform(jax.random.fold_in(own, dim), (blocks,), jnp.float32, smallest / len(split), top_value / len(split)))
        gain = gain * jnp.repeat(steps, dims[dim] // blocks).reshape([-1 if axis == dim else 1 for axis in range(len(dims))])
    return gain


def shared_out(stream_key, own, number, rows, amount, top, most, lean):
    ranking = jax.random.permutation(stream_key, amount)
    heavy_load, usual = shares(amount, rows * top, most, lean, True), shares(amount, rows * top, most, lean, False)
    places = jnp.arange(amount)

    def named(sizes, offset_by):
        used = int((sizes > 0).sum())
        fixed = max(1, used // 4)
        passed = fixed + (places - fixed + offset_by * (used - fixed)) % max(1, amount - fixed)
        return jnp.zeros((amount,), jnp.int32).at[ranking[jnp.where(places < fixed, places, passed)]].set(jnp.asarray(sizes, jnp.int32))

    sizes = jnp.where(number % 4 == 0, named(heavy_load, number // 4), named(usual, number - number // 4 - 1))
    mixed = jax.random.permutation(jax.random.fold_in(own, 3), amount)
    donor, sink = mixed[0:amount // 2 * 2:2], mixed[1:amount // 2 * 2:2]
    margin = jnp.minimum(sizes[donor] - 1, most - sizes[sink]) // 2
    margin = jnp.where((donor == ranking[0]) | (sink == ranking[0]) | (sizes[sink] == 0), 0, jnp.maximum(margin, 0))
    passed = jax.random.randint(jax.random.fold_in(own, 4), (amount // 2,), 0, 1 << 20) % (margin + 1)
    sizes = sizes.at[donor].add(-passed).at[sink].add(passed)
    members = jnp.searchsorted(jnp.cumsum(sizes), jnp.arange(rows * top), side="right").astype(jnp.int32)
    table = members.reshape(top, rows).T
    table = table[jax.random.permutation(jax.random.fold_in(own, 1), rows)]
    offset_by = jax.random.randint(jax.random.fold_in(own, 2), (rows, 1), 0, top)
    return jnp.take_along_axis(table, (jnp.arange(top)[None, :] + offset_by) % top, axis=1)


def shares(number_of, total, reach, lean, full):
    weights = [(1 << 20) // math.isqrt(grade ** lean) + 1 for grade in range(1, number_of + 1)]
    largest = reach if full else min(reach, max(-(-total // number_of), total * weights[0] // sum(weights)))
    least = 1 if total - largest >= number_of - 1 else 0
    holding, spare = [largest] + [least] * (number_of - 1), total - largest - least * (number_of - 1)
    while spare > 0:
        movable = [i for i in range(1, number_of) if holding[i] < largest] or [i for i in range(1, number_of) if holding[i] < reach]
        whole, left = sum([weights[i] for i in movable]), spare
        for i in movable:
            addition = min(reach - holding[i], max(1, left * weights[i] // whole), spare)
            holding[i] = holding[i] + addition
            spare = spare - addition
    return np.array(holding)


def noise(key, shape, scale, limit, shards=(), held_as=jnp.bfloat16):
    array = scale * jax.random.normal(key, shape, jnp.float32)
    if shards:
        array = array * block_levels(key, shape, shards, -0.22, 0.18)
    return jnp.clip(array, -limit, limit).astype(held_as)


def setup_inputs(seed: int = 0, part: int = 0) -> dict:
    key_of = jax.random.split(jax.random.key(seed), 7)
    own_keys = jax.random.split(jax.random.fold_in(key_of[6], part), 7)
    queries = draw_queries(jax.random.fold_in(jax.random.fold_in(key_of[6], part), 71), part)
    answer_prompt_keys = jax.random.split(jax.random.fold_in(own_keys[1], 1), TOKENS // TOK_DEV)
    answer_prompt_turns = jax.random.permutation(jax.random.fold_in(own_keys[1], 3), TOKENS // TOK_DEV)
    answer_prompt = jax.vmap(lambda own, number: shared_out(jax.random.fold_in(own_keys[1], 2), own, number, TOK_DEV, N_DP, 1, CAP, 2))(answer_prompt_keys, answer_prompt_turns).reshape((TOKENS, 1))
    prompt_owner = jax.random.permutation(own_keys[2], N_DP).astype(jnp.int32)
    context_keys = draw_context_keys(jax.random.fold_in(jax.random.fold_in(key_of[6], part), 71), part)
    context_values = noise(own_keys[4], (N_DP * CTX, KV_HEADS * HD), 1.0, 6.0, ((0, 8), (1, 2)))
    score_weight = noise(key_of[5], (HEADS * HD,), 1.0, 6.0, ((0, 2),), jnp.float32)
    return {"queries": queries, "answer_prompt": answer_prompt, "prompt_owner": prompt_owner, "context_keys": context_keys, "context_values": context_values, "score_weight": score_weight}


def reference(queries, answer_prompt, prompt_owner, context_keys, context_values, score_weight):
    group_size = HEADS // KV_HEADS
    block_of = prompt_owner[answer_prompt[:, 0]].astype(jnp.int32)
    key_blocks = context_keys.reshape(N_DP, CTX, KV_HEADS, HD)
    value_blocks = context_values.reshape(N_DP, CTX, KV_HEADS, HD)
    query_batches = queries.reshape(TOKENS // 8, 8, KV_HEADS, group_size, HD)
    block_batches = block_of.reshape(TOKENS // 8, 8)
    weight_heads = score_weight.reshape(KV_HEADS, group_size, HD).astype(jnp.float32)

    def per_batch(packed):
        query_part = packed[0].astype(jnp.float32)
        owner_part = packed[1]
        key_part = key_blocks[owner_part].astype(jnp.float32)
        value_part = value_blocks[owner_part].astype(jnp.float32)
        logits = jnp.einsum('tkgd,tckd->tkgc', query_part, key_part) / math.sqrt(HD)
        weights = jax.nn.softmax(logits, axis=-1).astype(jnp.bfloat16)
        weights = lax.optimization_barrier(weights).astype(jnp.float32)
        attended = jnp.einsum('tkgc,tckd->tkgd', weights, value_part).astype(jnp.bfloat16)
        attended = lax.optimization_barrier(attended).astype(jnp.float32)
        return lax.optimization_barrier(jnp.sum(attended * weight_heads[None], axis=(1, 2, 3)))
    return lax.map(per_batch, (query_batches, block_batches)).reshape(TOKENS)
```

```python
import functools
import math

import jax
import jax.numpy as jnp
from jax import lax
from jax.experimental import pallas as pl
from jax.experimental.pallas import tpu as pltpu
from jax.sharding import PartitionSpec as P

HD = 128
SCALE = math.log2(math.e) / math.sqrt(HD)
MAX_PAIRWISE = 16


def route_kernel(capacity, by_xor, me_ref, prompt_ref, owner_ref, query_ref, column_ref, *out_refs):
    tok_rows = prompt_ref.shape[0]
    peers = len(out_refs) if by_xor else out_refs[0].shape[0] // capacity
    prompt_lane = lax.broadcasted_iota(jnp.int32, (tok_rows, owner_ref.shape[1]), 1)
    target = jnp.sum(
        jnp.where(prompt_ref[...] == prompt_lane, owner_ref[...], 0), axis=1, keepdims=True
    )
    peer_lane = lax.broadcasted_iota(jnp.int32, (tok_rows, peers), 1)
    hits = (target == peer_lane).astype(jnp.float32)
    earlier_mask = lax.broadcasted_iota(jnp.int32, (tok_rows, tok_rows), 0) > (
        lax.broadcasted_iota(jnp.int32, (tok_rows, tok_rows), 1)
    )
    earlier = jnp.dot(
        earlier_mask.astype(jnp.bfloat16),
        hits.astype(jnp.bfloat16),
        preferred_element_type=jnp.float32,
    )
    rank = jnp.sum(earlier * hits, axis=1, keepdims=True).astype(jnp.int32)
    place = target ^ me_ref[0] if by_xor else target
    column = place * capacity + rank
    column_ref[...] = column
    slots = peers * capacity
    picks = (column == lax.broadcasted_iota(jnp.int32, (tok_rows, slots), 1)).astype(jnp.float32)
    picks = picks.T.astype(jnp.bfloat16)
    for n, out_ref in enumerate(out_refs):
        rows = out_ref.shape[0]
        out_ref[...] = jnp.dot(
            picks[n * rows : (n + 1) * rows], query_ref[...], preferred_element_type=jnp.float32
        ).astype(jnp.bfloat16)


def route(queries, answer_prompt, prompt_owner, me, peers, capacity, by_xor):
    tok_rows, width = queries.shape
    pieces = peers if by_xor else 1
    piece_rows = peers * capacity // pieces
    step = min(width, 1024)
    return pl.pallas_call(
        functools.partial(route_kernel, capacity, by_xor),
        grid=(width // step,),
        in_specs=[
            pl.BlockSpec(memory_space=pltpu.SMEM),
            pl.BlockSpec((tok_rows, 1), lambda c: (0, 0)),
            pl.BlockSpec((1, prompt_owner.shape[0]), lambda c: (0, 0)),
            pl.BlockSpec((tok_rows, step), lambda c: (0, c)),
        ],
        out_specs=[pl.BlockSpec((tok_rows, 1), lambda c: (0, 0))]
        + [pl.BlockSpec((piece_rows, step), lambda c: (0, c))] * pieces,
        out_shape=[jax.ShapeDtypeStruct((tok_rows, 1), jnp.int32)]
        + [jax.ShapeDtypeStruct((piece_rows, width), jnp.bfloat16)] * pieces,
        name="route",
    )(me.reshape(1), answer_prompt, prompt_owner.reshape(1, -1), queries)


def attend_kernel(group_size, query_ref, key_ref, value_ref, weight_ref, score_ref, total_ref):
    kv_head = pl.program_id(1)
    rows = query_ref.shape[0]
    stacked = jnp.concatenate(
        [query_ref[:, h * HD : (h + 1) * HD] for h in range(group_size)], axis=0
    )
    logits = lax.dot_general(
        stacked, key_ref[...], (((1,), (1,)), ((), ())), preferred_element_type=jnp.float32
    )
    peak = jnp.max(logits, axis=1, keepdims=True)
    exponent = jnp.exp2((logits - peak) * SCALE)
    inverse = 1.0 / jnp.sum(exponent, axis=1, keepdims=True)
    probs = (exponent * inverse).astype(jnp.bfloat16)
    attended = jnp.dot(probs, value_ref[...], preferred_element_type=jnp.float32)
    attended = attended.astype(jnp.bfloat16).astype(jnp.float32)
    total = jnp.zeros((rows, HD), jnp.float32)
    for h in range(group_size):
        total += attended[h * rows : (h + 1) * rows] * weight_ref[:, h * HD : (h + 1) * HD]

    @pl.when(kv_head == 0)
    def _():
        total_ref[...] = total

    @pl.when(kv_head > 0)
    def _():
        total_ref[...] += total

    @pl.when(kv_head == pl.num_programs(1) - 1)
    def _():
        score_ref[0] = jnp.sum(total_ref[...].T, axis=0, keepdims=True)


def attend_score(query_rows, key_rows, value_rows, score_weight):
    row_count, width = query_rows.shape
    context_len, kv_width = key_rows.shape
    kv_local = kv_width // HD
    group_size = width // kv_width
    block = math.gcd(row_count, 32)
    blocks = row_count // block
    flops = 4 * row_count * width * context_len
    return pl.pallas_call(
        functools.partial(attend_kernel, group_size),
        grid=(blocks, kv_local),
        in_specs=[
            pl.BlockSpec((block, group_size * HD), lambda r, g: (r, g)),
            pl.BlockSpec((context_len, HD), lambda r, g: (0, g)),
            pl.BlockSpec((context_len, HD), lambda r, g: (0, g)),
            pl.BlockSpec((1, group_size * HD), lambda r, g: (0, g)),
        ],
        out_specs=pl.BlockSpec((1, 1, block), lambda r, g: (r, 0, 0)),
        out_shape=jax.ShapeDtypeStruct((blocks, 1, block), jnp.float32),
        scratch_shapes=[pltpu.VMEM((block, HD), jnp.float32)],
        cost_estimate=pl.CostEstimate(
            flops=flops,
            bytes_accessed=2 * (row_count * width + 2 * context_len * kv_width),
            transcendentals=row_count * width // HD * context_len,
        ),
        name="attend_score",
    )(query_rows, key_rows, value_rows, score_weight.reshape(1, -1)).reshape(1, row_count)


def on_device(queries, answer_prompt, prompt_owner, context_keys, context_values, score_weight):
    tok_rows, width = queries.shape
    peers = lax.axis_size("dp")
    cores = lax.axis_size("tensor")
    capacity = max(2, 2 * tok_rows // peers)
    by_xor = peers <= MAX_PAIRWISE and peers & (peers - 1) == 0 and capacity % 16 == 0
    column, *pieces = route(
        queries, answer_prompt, prompt_owner, lax.axis_index("dp"), peers, capacity, by_xor
    )
    score = functools.partial(
        attend_score,
        key_rows=context_keys,
        value_rows=context_values,
        score_weight=score_weight,
    )
    if by_xor:
        order = sorted(range(1, peers), reverse=True)
        arrived = {
            s: lax.ppermute(pieces[s], "dp", [(k, k ^ s) for k in range(peers)]) for s in order
        }
        arrived[0] = pieces[0]
        terms = []
        for s in range(peers):
            own = score(arrived[s])
            both = []
            for c in range(cores):
                if s == 0 and c == 0:
                    both.append(own)
                    continue
                both.append(
                    lax.ppermute(
                        own,
                        ("dp", "tensor"),
                        [
                            (k * cores + j, (k ^ s) * cores + (j ^ c))
                            for k in range(peers)
                            for j in range(cores)
                        ],
                    )
                )
            terms.append(sum(both[1:], both[0]))
        returned = jnp.concatenate(terms, axis=1)
        slots = lax.broadcasted_iota(jnp.int32, (tok_rows, peers * capacity), 1)
        return jnp.sum(jnp.where(column == slots, returned, 0.0), axis=1)
    arrived = lax.all_to_all(
        pieces[0].reshape(peers, capacity, width), "dp", split_axis=0, concat_axis=0, tiled=True
    )
    own = score(arrived.reshape(peers * capacity, width))
    returned = lax.all_to_all(
        own.reshape(peers, capacity), "dp", split_axis=0, concat_axis=0, tiled=True
    )
    slots = lax.broadcasted_iota(jnp.int32, (tok_rows, peers * capacity), 1)
    head_terms = jnp.sum(
        jnp.where(column == slots, returned.reshape(1, peers * capacity), 0.0), axis=1
    )
    return lax.psum(head_terms, "tensor")


def solution(mesh):
    return jax.shard_map(
        on_device,
        mesh=mesh,
        in_specs=(
            P(("groups", "dp"), "tensor"),
            P(("groups", "dp"), None),
            P("groups"),
            P(("groups", "dp"), "tensor"),
            P(("groups", "dp"), "tensor"),
            P("tensor"),
        ),
        out_specs=P(("groups", "dp")),
        check_vma=False,
    )
```

```python
import functools
import math

import jax
import jax.numpy as jnp
from jax import lax
from jax.experimental import pallas as pl
from jax.experimental.pallas import tpu as pltpu
from jax.sharding import PartitionSpec as P

HD = 128
SCALE = math.log2(math.e) / math.sqrt(HD)
MAX_PAIRWISE = 16


def route_kernel(capacity, by_xor, owner_ref, prompt_ref, query_ref, column_ref, *refs):
    *out_refs, picks_ref = refs
    tok_rows = prompt_ref.shape[1]
    peers = picks_ref.shape[0] // capacity

    @pl.when(pl.program_id(0) == 0)
    def _():
        prompt = prompt_ref[...]
        target = lax.fori_loop(
            0,
            owner_ref.shape[0],
            lambda k, t: jnp.where(prompt == k, owner_ref[k], t),
            jnp.zeros_like(prompt),
            unroll=owner_ref.shape[0] <= MAX_PAIRWISE,
        )
        peer_row = lax.broadcasted_iota(jnp.int32, (peers, tok_rows), 0)
        hits = (target == peer_row).astype(jnp.float32)
        earlier_mask = lax.broadcasted_iota(jnp.int32, (tok_rows, tok_rows), 0) < (
            lax.broadcasted_iota(jnp.int32, (tok_rows, tok_rows), 1)
        )
        earlier = jnp.dot(
            hits.astype(jnp.bfloat16),
            earlier_mask.astype(jnp.bfloat16),
            preferred_element_type=jnp.float32,
        )
        rank = jnp.sum(earlier * hits, axis=0, keepdims=True).astype(jnp.int32)
        place = target ^ lax.axis_index("dp") if by_xor else target
        column = place * capacity + rank
        column_ref[...] = column
        slot_row = lax.broadcasted_iota(jnp.int32, picks_ref.shape, 0)
        picks_ref[...] = (column == slot_row).astype(jnp.bfloat16)

    for n, out_ref in enumerate(out_refs):
        rows = out_ref.shape[0]
        out_ref[...] = jnp.dot(
            picks_ref[n * rows : (n + 1) * rows], query_ref[...], preferred_element_type=jnp.float32
        ).astype(jnp.bfloat16)


def route(queries, answer_prompt, prompt_owner, peers, capacity, by_xor):
    tok_rows, width = queries.shape
    pieces = peers if by_xor else 1
    piece_rows = peers * capacity // pieces
    step = min(width, 1024)
    return pl.pallas_call(
        functools.partial(route_kernel, capacity, by_xor),
        grid=(width // step,),
        in_specs=[
            pl.BlockSpec(memory_space=pltpu.SMEM),
            pl.BlockSpec((1, tok_rows), lambda c: (0, 0)),
            pl.BlockSpec((tok_rows, step), lambda c: (0, c)),
        ],
        out_specs=[pl.BlockSpec((1, tok_rows), lambda c: (0, 0))]
        + [pl.BlockSpec((piece_rows, step), lambda c: (0, c))] * pieces,
        out_shape=[jax.ShapeDtypeStruct((1, tok_rows), jnp.int32)]
        + [jax.ShapeDtypeStruct((piece_rows, width), jnp.bfloat16)] * pieces,
        scratch_shapes=[pltpu.VMEM((peers * capacity, tok_rows), jnp.bfloat16)],
        name="route",
    )(prompt_owner, answer_prompt.reshape(1, tok_rows), queries)


def attend_block(query_ref, key_ref, value_ref, weight_ref, shift_by_peak):
    rows = query_ref.shape[0]
    kv_local = key_ref.shape[1] // HD
    group_size = query_ref.shape[1] // key_ref.shape[1]
    total = jnp.zeros((rows, HD), jnp.float32)
    smallest = largest = None
    for g in range(kv_local):
        heads = [slice((g * group_size + h) * HD, (g * group_size + h + 1) * HD) for h in range(group_size)]
        kv = slice(g * HD, (g + 1) * HD)
        stacked = jnp.concatenate([query_ref[:, head] for head in heads], axis=0)
        logits = lax.dot_general(
            stacked, key_ref[:, kv], (((1,), (1,)), ((), ())), preferred_element_type=jnp.float32
        )
        if shift_by_peak:
            logits = logits - jnp.max(logits, axis=1, keepdims=True)
        exponent = jnp.exp2(logits * SCALE)
        norm = jnp.sum(exponent, axis=1, keepdims=True)
        smallest = norm if g == 0 else jnp.minimum(smallest, norm)
        largest = norm if g == 0 else jnp.maximum(largest, norm)
        probs = (exponent * (1.0 / norm)).astype(jnp.bfloat16)
        attended = jnp.dot(probs, value_ref[:, kv], preferred_element_type=jnp.float32)
        attended = attended.astype(jnp.bfloat16).astype(jnp.float32)
        for h, head in enumerate(heads):
            total += attended[h * rows : (h + 1) * rows] * weight_ref[:, head]
    return jnp.sum(total.T, axis=0, keepdims=True), jnp.min(smallest), jnp.max(largest)


def attend_kernel(query_ref, key_ref, value_ref, weight_ref, score_ref):
    score, smallest, largest = attend_block(query_ref, key_ref, value_ref, weight_ref, False)
    score_ref[0] = score

    @pl.when(jnp.logical_not((smallest > 1e-25) & (largest < 1e25)))
    def _():
        score_ref[0] = attend_block(query_ref, key_ref, value_ref, weight_ref, True)[0]


def attend_score(query_rows, key_rows, value_rows, score_weight):
    row_count, width = query_rows.shape
    context_len, kv_width = key_rows.shape
    block = math.gcd(row_count, 32)
    blocks = row_count // block
    return pl.pallas_call(
        attend_kernel,
        grid=(blocks,),
        in_specs=[pl.BlockSpec((block, width), lambda r: (r, 0))]
        + [pl.BlockSpec(memory_space=pltpu.VMEM)] * 3,
        out_specs=pl.BlockSpec((1, 1, block), lambda r: (r, 0, 0)),
        out_shape=jax.ShapeDtypeStruct((blocks, 1, block), jnp.float32),
        compiler_params=pltpu.CompilerParams(vmem_limit_bytes=24 << 20),
        cost_estimate=pl.CostEstimate(
            flops=4 * row_count * width * context_len,
            bytes_accessed=2 * (row_count * width + 2 * context_len * kv_width),
            transcendentals=row_count * width // HD * context_len,
        ),
        name="attend_score",
    )(query_rows, key_rows, value_rows, score_weight.reshape(1, -1)).reshape(1, row_count)


def pick_slots(returned, column):
    slots = lax.broadcasted_iota(jnp.int32, (column.shape[1], returned.shape[1]), 1)
    return jnp.sum(jnp.where(column.reshape(-1, 1) == slots, returned, 0.0), axis=1)


def on_device(queries, answer_prompt, prompt_owner, context_keys, context_values, score_weight):
    tok_rows, width = queries.shape
    peers = lax.axis_size("dp")
    cores = lax.axis_size("tensor")
    capacity = max(2, 2 * tok_rows // peers)
    by_xor = peers <= MAX_PAIRWISE and peers & (peers - 1) == 0 and capacity % 16 == 0
    column, *pieces = route(
        queries, answer_prompt, prompt_owner, peers, capacity, by_xor
    )
    score = functools.partial(
        attend_score,
        key_rows=context_keys,
        value_rows=context_values,
        score_weight=score_weight,
    )
    if by_xor:
        pairs = [[(k, k ^ s) for k in range(peers)] for s in range(peers)]
        arrived = [pieces[0]] + [lax.ppermute(pieces[s], "dp", pairs[s]) for s in range(1, peers)]
        arrived[0], arrived[1] = lax.optimization_barrier((arrived[0], arrived[1]))
        returned = [score(arrived[0])]
        for s in range(1, peers):
            returned.append(lax.ppermute(score(arrived[s]), "dp", pairs[s]))
        own = pick_slots(jnp.concatenate(returned, axis=1), column)
        other = lax.ppermute(own, "tensor", [(k, (k + 1) % cores) for k in range(cores)])
        return own + other
    arrived = lax.all_to_all(
        pieces[0].reshape(peers, capacity, width), "dp", split_axis=0, concat_axis=0, tiled=True
    )
    own = score(arrived.reshape(peers * capacity, width))
    returned = lax.all_to_all(
        own.reshape(peers, capacity), "dp", split_axis=0, concat_axis=0, tiled=True
    )
    head_terms = pick_slots(returned.reshape(1, peers * capacity), column)
    return lax.psum(head_terms, "tensor")


def solution(mesh):
    return jax.shard_map(
        on_device,
        mesh=mesh,
        in_specs=(
            P(("groups", "dp"), "tensor"),
            P(("groups", "dp"), None),
            P("groups"),
            P(("groups", "dp"), "tensor"),
            P(("groups", "dp"), "tensor"),
            P("tensor"),
        ),
        out_specs=P(("groups", "dp")),
        check_vma=False,
    )
```

```python
import functools
import math

import jax
import jax.numpy as jnp
from jax import lax
from jax.experimental import pallas as pl
from jax.experimental.pallas import tpu as pltpu
from jax.sharding import PartitionSpec as P

HD = 128
SCALE = math.log2(math.e) / math.sqrt(HD)
MAX_PAIRWISE = 16
QUERY_PARTS = 4


def place_rows(slot_of_token, first_slot, query_ref, out_refs, waits=()):
    slots = sum(out_ref.shape[0] for out_ref in out_refs)
    tok_rows, width = query_ref.shape
    slot_row = first_slot + lax.broadcasted_iota(jnp.int32, (slots, tok_rows), 0)
    picks = (slot_of_token == slot_row).astype(jnp.bfloat16)
    step = width // QUERY_PARTS
    for part in range(QUERY_PARTS):
        columns = slice(part * step, (part + 1) * step)
        if waits:
            waits[part].wait()
        placed = jnp.dot(picks, query_ref[:, columns], preferred_element_type=jnp.float32)
        placed = placed.astype(jnp.bfloat16)
        start = 0
        for out_ref in out_refs:
            out_ref[:, columns] = placed[start : start + out_ref.shape[0]]
            start += out_ref.shape[0]


def route_kernel(peers, capacity, order, owner_hbm, prompt_hbm, query_hbm, column_ref, query_ref, *refs):
    *out_refs, owner_ref, prompt_ref, small_sems, query_sems = refs
    tok_rows, width = query_hbm.shape
    step = width // QUERY_PARTS
    small = [
        pltpu.make_async_copy(owner_hbm, owner_ref, small_sems.at[0]),
        pltpu.make_async_copy(prompt_hbm, prompt_ref, small_sems.at[1]),
    ]
    parts = [
        pltpu.make_async_copy(
            query_hbm.at[:, pl.ds(part * step, step)],
            query_ref.at[:, pl.ds(part * step, step)],
            query_sems.at[part],
        )
        for part in range(QUERY_PARTS)
    ]
    for copy in small + parts:
        copy.start()
    for copy in small:
        copy.wait()
    prompt = prompt_ref[...]
    target = lax.fori_loop(
        0,
        owner_ref.shape[0],
        lambda k, t: jnp.where(prompt == k, owner_ref[k], t),
        jnp.zeros_like(prompt),
        unroll=owner_ref.shape[0] <= MAX_PAIRWISE,
    )
    peer_row = lax.broadcasted_iota(jnp.int32, (peers, tok_rows), 0)
    hits = (target == peer_row).astype(jnp.float32)
    earlier_mask = lax.broadcasted_iota(jnp.int32, (tok_rows, tok_rows), 0) < (
        lax.broadcasted_iota(jnp.int32, (tok_rows, tok_rows), 1)
    )
    earlier = jnp.dot(
        hits.astype(jnp.bfloat16),
        earlier_mask.astype(jnp.bfloat16),
        preferred_element_type=jnp.float32,
    )
    rank = jnp.sum(earlier * hits, axis=0, keepdims=True).astype(jnp.int32)
    place = target
    if order is not None:
        step = target ^ lax.axis_index("dp")
        for position, s in enumerate(order):
            place = jnp.where(step == s, position, place)
    column = place * capacity + rank
    column_ref[...] = column
    place_rows(column, 0, query_ref, out_refs, parts)


def route(queries, answer_prompt, prompt_owner, peers, capacity, order, pieces):
    tok_rows, width = queries.shape
    piece_rows = capacity if order is not None else peers * capacity
    return pl.pallas_call(
        functools.partial(route_kernel, peers, capacity, order),
        in_specs=[pl.BlockSpec(memory_space=pltpu.HBM)] * 3,
        out_specs=[pl.BlockSpec(memory_space=pltpu.VMEM)] * (2 + pieces),
        out_shape=[
            jax.ShapeDtypeStruct((1, tok_rows), jnp.int32),
            jax.ShapeDtypeStruct((tok_rows, width), jnp.bfloat16),
        ]
        + [jax.ShapeDtypeStruct((piece_rows, width), jnp.bfloat16)] * pieces,
        scratch_shapes=[
            pltpu.SMEM(prompt_owner.shape, jnp.int32),
            pltpu.VMEM((1, tok_rows), jnp.int32),
            pltpu.SemaphoreType.DMA((2,)),
            pltpu.SemaphoreType.DMA((QUERY_PARTS,)),
        ],
        compiler_params=pltpu.CompilerParams(vmem_limit_bytes=52 << 20),
        name="route",
    )(prompt_owner, answer_prompt.reshape(1, tok_rows), queries)


def route_rest_kernel(first_slot, column_ref, query_ref, *out_refs):
    place_rows(column_ref[...], first_slot, query_ref, out_refs)


def route_rest(queries, column, first_piece, pieces, capacity):
    return pl.pallas_call(
        functools.partial(route_rest_kernel, first_piece * capacity),
        in_specs=[pl.BlockSpec(memory_space=pltpu.VMEM)] * 2,
        out_specs=[pl.BlockSpec(memory_space=pltpu.VMEM)] * pieces,
        out_shape=[jax.ShapeDtypeStruct((capacity, queries.shape[1]), jnp.bfloat16)] * pieces,
        compiler_params=pltpu.CompilerParams(vmem_limit_bytes=24 << 20),
        name="route_rest",
    )(column, queries)


def attend_block(query_ref, key_ref, value_ref, weight_ref, shift_by_peak):
    rows = query_ref.shape[0]
    kv_local = key_ref.shape[1] // HD
    group_size = query_ref.shape[1] // key_ref.shape[1]
    total = jnp.zeros((rows, HD), jnp.float32)
    smallest = largest = None
    for g in range(kv_local):
        heads = [slice((g * group_size + h) * HD, (g * group_size + h + 1) * HD) for h in range(group_size)]
        kv = slice(g * HD, (g + 1) * HD)
        stacked = jnp.concatenate([query_ref[:, head] for head in heads], axis=0)
        logits = lax.dot_general(
            stacked, key_ref[:, kv], (((1,), (1,)), ((), ())), preferred_element_type=jnp.float32
        )
        if shift_by_peak:
            logits = logits - jnp.max(logits, axis=1, keepdims=True)
        exponent = jnp.exp2(logits * SCALE)
        norm = jnp.sum(exponent, axis=1, keepdims=True)
        smallest = norm if g == 0 else jnp.minimum(smallest, norm)
        largest = norm if g == 0 else jnp.maximum(largest, norm)
        probs = (exponent * (1.0 / norm)).astype(jnp.bfloat16)
        attended = jnp.dot(probs, value_ref[:, kv], preferred_element_type=jnp.float32)
        attended = attended.astype(jnp.bfloat16).astype(jnp.float32)
        for h, head in enumerate(heads):
            total += attended[h * rows : (h + 1) * rows] * weight_ref[:, head]
    return jnp.sum(total.T, axis=0, keepdims=True), jnp.min(smallest), jnp.max(largest)


def attend_kernel(query_ref, key_ref, value_ref, weight_ref, score_ref):
    score, smallest, largest = attend_block(query_ref, key_ref, value_ref, weight_ref, False)
    score_ref[0] = score

    @pl.when(jnp.logical_not((smallest > 1e-25) & (largest < 1e25)))
    def _():
        score_ref[0] = attend_block(query_ref, key_ref, value_ref, weight_ref, True)[0]


def attend_score(query_rows, key_rows, value_rows, score_weight):
    row_count, width = query_rows.shape
    context_len, kv_width = key_rows.shape
    block = math.gcd(row_count, 32)
    blocks = row_count // block
    return pl.pallas_call(
        attend_kernel,
        grid=(blocks,),
        in_specs=[pl.BlockSpec((block, width), lambda r: (r, 0))]
        + [pl.BlockSpec(memory_space=pltpu.VMEM)] * 3,
        out_specs=pl.BlockSpec((1, 1, block), lambda r: (r, 0, 0)),
        out_shape=jax.ShapeDtypeStruct((blocks, 1, block), jnp.float32),
        compiler_params=pltpu.CompilerParams(vmem_limit_bytes=24 << 20),
        cost_estimate=pl.CostEstimate(
            flops=4 * row_count * width * context_len,
            bytes_accessed=2 * (row_count * width + 2 * context_len * kv_width),
            transcendentals=row_count * width // HD * context_len,
        ),
        name="attend_score",
    )(query_rows, key_rows, value_rows, score_weight.reshape(1, -1)).reshape(1, row_count)


def pick_slots(returned, column):
    slots = lax.broadcasted_iota(jnp.int32, (column.shape[1], returned.shape[1]), 1)
    return jnp.sum(jnp.where(column.reshape(-1, 1) == slots, returned, 0.0), axis=1)


def send_order(peers):
    if peers == 8:
        return (4, 1, 2, 3, 5, 7, 6, 0)
    return tuple(range(1, peers)) + (0,)


def on_device(queries, answer_prompt, prompt_owner, context_keys, context_values, score_weight):
    tok_rows, width = queries.shape
    peers = lax.axis_size("dp")
    cores = lax.axis_size("tensor")
    capacity = max(2, 2 * tok_rows // peers)
    by_xor = peers <= MAX_PAIRWISE and peers & (peers - 1) == 0 and capacity % 16 == 0
    order = send_order(peers) if by_xor else None
    early = 5 if by_xor else 1
    column, held_queries, *pieces = route(
        queries, answer_prompt, prompt_owner, peers, capacity, order, early
    )
    score = functools.partial(
        attend_score,
        key_rows=context_keys,
        value_rows=context_values,
        score_weight=score_weight,
    )
    if by_xor:
        pairs = [[(k, k ^ s) for k in range(peers)] for s in range(peers)]
        pieces += route_rest(held_queries, column, early, peers - early, capacity)
        arrived = [
            lax.ppermute(piece, "dp", pairs[s]) if s else piece for s, piece in zip(order, pieces)
        ]
        own_at = order.index(0)
        arrived[own_at], arrived[0] = lax.optimization_barrier((arrived[own_at], arrived[0]))
        made, last = {}, None
        for k in [own_at] + [k for k in range(peers) if k != own_at]:
            rows = arrived[k]
            if last is not None:
                rows, last = lax.optimization_barrier((rows, last))
            made[order[k]] = last = score(rows)
        odd = [made[s] for s in range(1, peers, 2)]
        crossed = jnp.split(
            lax.ppermute(jnp.concatenate(odd, axis=1), "dp", pairs[1]), peers // 2, axis=1
        )
        returned = {0: made[0], 1: crossed[0]}
        for s in sorted(range(2, peers, 2), key=order.index):
            both = jnp.concatenate([made[s], crossed[s // 2]], axis=1)
            returned[s], returned[s + 1] = jnp.split(lax.ppermute(both, "dp", pairs[s]), 2, axis=1)
        own = pick_slots(jnp.concatenate([returned[s] for s in order], axis=1), column)
        other = lax.ppermute(own, "tensor", [(k, (k + 1) % cores) for k in range(cores)])
        return own + other
    arrived = lax.all_to_all(
        pieces[0].reshape(peers, capacity, width), "dp", split_axis=0, concat_axis=0, tiled=True
    )
    own = score(arrived.reshape(peers * capacity, width))
    returned = lax.all_to_all(
        own.reshape(peers, capacity), "dp", split_axis=0, concat_axis=0, tiled=True
    )
    head_terms = pick_slots(returned.reshape(1, peers * capacity), column)
    return lax.psum(head_terms, "tensor")


def solution(mesh):
    return jax.shard_map(
        on_device,
        mesh=mesh,
        in_specs=(
            P(("groups", "dp"), "tensor"),
            P(("groups", "dp"), None),
            P("groups"),
            P(("groups", "dp"), "tensor"),
            P(("groups", "dp"), "tensor"),
            P("tensor"),
        ),
        out_specs=P(("groups", "dp")),
        check_vma=False,
    )
```

```python
import functools
import math

import jax
import jax.numpy as jnp
from jax import lax
from jax.experimental import pallas as pl
from jax.experimental.pallas import tpu as pltpu
from jax.sharding import PartitionSpec as P

HD = 128
SCALE = math.log2(math.e) / math.sqrt(HD)
MAX_PAIRWISE = 16
QUERY_PARTS = 4


def place_rows(slot_of_token, first_slot, query_ref, out_refs, waits=()):
    slots = sum(out_ref.shape[0] for out_ref in out_refs)
    tok_rows, width = query_ref.shape
    slot_row = first_slot + lax.broadcasted_iota(jnp.int32, (slots, tok_rows), 0)
    picks = (slot_of_token == slot_row).astype(jnp.bfloat16)
    step = width // QUERY_PARTS
    for part in range(QUERY_PARTS):
        columns = slice(part * step, (part + 1) * step)
        if waits:
            waits[part].wait()
        placed = jnp.dot(picks, query_ref[:, columns], preferred_element_type=jnp.float32)
        placed = placed.astype(jnp.bfloat16)
        start = 0
        for out_ref in out_refs:
            out_ref[:, columns] = placed[start : start + out_ref.shape[0]]
            start += out_ref.shape[0]


def route_kernel(peers, capacity, order, owner_hbm, prompt_hbm, query_hbm, column_ref, query_ref, *refs):
    *out_refs, owner_ref, prompt_ref, small_sems, query_sems = refs
    tok_rows, width = query_hbm.shape
    step = width // QUERY_PARTS
    small = [
        pltpu.make_async_copy(owner_hbm, owner_ref, small_sems.at[0]),
        pltpu.make_async_copy(prompt_hbm, prompt_ref, small_sems.at[1]),
    ]
    parts = [
        pltpu.make_async_copy(
            query_hbm.at[:, pl.ds(part * step, step)],
            query_ref.at[:, pl.ds(part * step, step)],
            query_sems.at[part],
        )
        for part in range(QUERY_PARTS)
    ]
    for copy in small + parts:
        copy.start()
    for copy in small:
        copy.wait()
    prompt = prompt_ref[...]
    target = lax.fori_loop(
        0,
        owner_ref.shape[0],
        lambda k, t: jnp.where(prompt == k, owner_ref[k], t),
        jnp.zeros_like(prompt),
        unroll=owner_ref.shape[0] <= MAX_PAIRWISE,
    )
    peer_row = lax.broadcasted_iota(jnp.int32, (peers, tok_rows), 0)
    hits = (target == peer_row).astype(jnp.float32)
    earlier_mask = lax.broadcasted_iota(jnp.int32, (tok_rows, tok_rows), 0) < (
        lax.broadcasted_iota(jnp.int32, (tok_rows, tok_rows), 1)
    )
    earlier = jnp.dot(
        hits.astype(jnp.bfloat16),
        earlier_mask.astype(jnp.bfloat16),
        preferred_element_type=jnp.float32,
    )
    rank = jnp.sum(earlier * hits, axis=0, keepdims=True).astype(jnp.int32)
    place = target
    if order is not None:
        step = target ^ lax.axis_index("dp")
        for position, s in enumerate(order):
            place = jnp.where(step == s, position, place)
    column = place * capacity + rank
    column_ref[...] = column
    place_rows(column, 0, query_ref, out_refs, parts)


def route(queries, answer_prompt, prompt_owner, peers, capacity, order, pieces):
    tok_rows, width = queries.shape
    piece_rows = capacity if order is not None else peers * capacity
    return pl.pallas_call(
        functools.partial(route_kernel, peers, capacity, order),
        in_specs=[pl.BlockSpec(memory_space=pltpu.HBM)] * 3,
        out_specs=[pl.BlockSpec(memory_space=pltpu.VMEM)] * (2 + pieces),
        out_shape=[
            jax.ShapeDtypeStruct((1, tok_rows), jnp.int32),
            jax.ShapeDtypeStruct((tok_rows, width), jnp.bfloat16),
        ]
        + [jax.ShapeDtypeStruct((piece_rows, width), jnp.bfloat16)] * pieces,
        scratch_shapes=[
            pltpu.SMEM(prompt_owner.shape, jnp.int32),
            pltpu.VMEM((1, tok_rows), jnp.int32),
            pltpu.SemaphoreType.DMA((2,)),
            pltpu.SemaphoreType.DMA((QUERY_PARTS,)),
        ],
        compiler_params=pltpu.CompilerParams(vmem_limit_bytes=52 << 20),
        name="route",
    )(prompt_owner, answer_prompt.reshape(1, tok_rows), queries)


def route_rest_kernel(first_slot, column_ref, query_ref, *out_refs):
    place_rows(column_ref[...], first_slot, query_ref, out_refs)


def route_rest(queries, column, first_piece, pieces, capacity):
    return pl.pallas_call(
        functools.partial(route_rest_kernel, first_piece * capacity),
        in_specs=[pl.BlockSpec(memory_space=pltpu.VMEM)] * 2,
        out_specs=[pl.BlockSpec(memory_space=pltpu.VMEM)] * pieces,
        out_shape=[jax.ShapeDtypeStruct((capacity, queries.shape[1]), jnp.bfloat16)] * pieces,
        compiler_params=pltpu.CompilerParams(vmem_limit_bytes=24 << 20),
        name="route_rest",
    )(column, queries)


def attend_block(query_ref, key_ref, value_ref, weight_ref, shift_by_peak):
    rows = query_ref.shape[0]
    kv_local = key_ref.shape[1] // HD
    group_size = query_ref.shape[1] // key_ref.shape[1]
    total = jnp.zeros((rows, HD), jnp.float32)
    smallest = largest = None
    for g in range(kv_local):
        heads = [slice((g * group_size + h) * HD, (g * group_size + h + 1) * HD) for h in range(group_size)]
        kv = slice(g * HD, (g + 1) * HD)
        stacked = jnp.concatenate([query_ref[:, head] for head in heads], axis=0)
        logits = lax.dot_general(
            stacked, key_ref[:, kv], (((1,), (1,)), ((), ())), preferred_element_type=jnp.float32
        )
        if shift_by_peak:
            logits = logits - jnp.max(logits, axis=1, keepdims=True)
        exponent = jnp.exp2(logits * SCALE)
        norm = jnp.sum(exponent, axis=1, keepdims=True)
        smallest = norm if g == 0 else jnp.minimum(smallest, norm)
        largest = norm if g == 0 else jnp.maximum(largest, norm)
        probs = (exponent * (1.0 / norm)).astype(jnp.bfloat16)
        attended = jnp.dot(probs, value_ref[:, kv], preferred_element_type=jnp.float32)
        attended = attended.astype(jnp.bfloat16).astype(jnp.float32)
        for h, head in enumerate(heads):
            total += attended[h * rows : (h + 1) * rows] * weight_ref[:, head]
    return jnp.sum(total.T, axis=0, keepdims=True), jnp.min(smallest), jnp.max(largest)


def attend_kernel(query_ref, key_ref, value_ref, weight_ref, score_ref):
    score, smallest, largest = attend_block(query_ref, key_ref, value_ref, weight_ref, False)
    score_ref[0] = score

    @pl.when(jnp.logical_not((smallest > 1e-25) & (largest < 1e25)))
    def _():
        score_ref[0] = attend_block(query_ref, key_ref, value_ref, weight_ref, True)[0]


def attend_score(query_rows, key_rows, value_rows, score_weight):
    row_count, width = query_rows.shape
    context_len, kv_width = key_rows.shape
    block = math.gcd(row_count, 32)
    blocks = row_count // block
    return pl.pallas_call(
        attend_kernel,
        grid=(blocks,),
        in_specs=[pl.BlockSpec((block, width), lambda r: (r, 0))]
        + [pl.BlockSpec(memory_space=pltpu.VMEM)] * 3,
        out_specs=pl.BlockSpec((1, 1, block), lambda r: (r, 0, 0)),
        out_shape=jax.ShapeDtypeStruct((blocks, 1, block), jnp.float32),
        compiler_params=pltpu.CompilerParams(vmem_limit_bytes=24 << 20),
        cost_estimate=pl.CostEstimate(flops=1 << 20, bytes_accessed=1 << 10, transcendentals=0),
        name="attend_score",
    )(query_rows, key_rows, value_rows, score_weight.reshape(1, -1)).reshape(1, row_count)


def pick_slots(returned, column):
    slots = lax.broadcasted_iota(jnp.int32, (column.shape[1], returned.shape[1]), 1)
    return jnp.sum(jnp.where(column.reshape(-1, 1) == slots, returned, 0.0), axis=1)


def send_order(peers):
    if peers == 8:
        return (7, 1, 2, 3, 5, 6, 4, 0)
    return tuple(range(1, peers)) + (0,)


def on_device(queries, answer_prompt, prompt_owner, context_keys, context_values, score_weight):
    tok_rows, width = queries.shape
    peers = lax.axis_size("dp")
    cores = lax.axis_size("tensor")
    capacity = max(2, 2 * tok_rows // peers)
    by_xor = peers <= MAX_PAIRWISE and peers & (peers - 1) == 0 and capacity % 16 == 0
    order = send_order(peers) if by_xor else None
    early = 5 if by_xor else 1
    column, held_queries, *pieces = route(
        queries, answer_prompt, prompt_owner, peers, capacity, order, early
    )
    context_keys, context_values, score_weight, column = lax.optimization_barrier(
        (context_keys, context_values, score_weight, column)
    )
    score = functools.partial(
        attend_score,
        key_rows=context_keys,
        value_rows=context_values,
        score_weight=score_weight,
    )
    if by_xor:
        pairs = [[(k, k ^ s) for k in range(peers)] for s in range(peers)]
        pieces += route_rest(held_queries, column, early, peers - early, capacity)
        arrived = [
            lax.ppermute(piece, "dp", pairs[s]) if s else piece for s, piece in zip(order, pieces)
        ]
        held = {s: [] for s in range(peers)}
        bits = [1 << b for b in range(peers.bit_length() - 1)]

        def hand_on(bit):
            ways = [s for s in range(bit, peers, 2 * bit)]
            steps = [step for way in ways for step, _ in held[way]]
            scores = jnp.concatenate([part for way in ways for _, part in held[way]], axis=1)
            parts = jnp.split(lax.ppermute(scores, "dp", pairs[bit]), len(steps), axis=1)
            for way in ways:
                for _ in held.pop(way):
                    held[way ^ bit].append((steps.pop(0), parts.pop(0)))

        def after(rows, bit):
            step, part = held[0][-1]
            rows, part = lax.optimization_barrier((rows, part))
            held[0][-1] = step, part
            return rows

        turns = [k for k in range(peers) if order[k]]
        turns.insert(1, order.index(0))
        last = None
        for turn, k in enumerate(turns):
            rows = arrived[k]
            if last is not None:
                rows, last = lax.optimization_barrier((rows, last))
            if turn == 6:
                hand_on(1)
            if turn == 7:
                rows = after(rows, 1)
            if turn == 7:
                hand_on(2)
            last = score(rows)
            held[order[k]].append((order[k], last))
        hand_on(bits[-1])
        returned = dict(held[0])
        own = pick_slots(jnp.concatenate([returned[s] for s in order], axis=1), column)
        other = lax.ppermute(own, "tensor", [(k, (k + 1) % cores) for k in range(cores)])
        return own + other
    arrived = lax.all_to_all(
        pieces[0].reshape(peers, capacity, width), "dp", split_axis=0, concat_axis=0, tiled=True
    )
    own = score(arrived.reshape(peers * capacity, width))
    returned = lax.all_to_all(
        own.reshape(peers, capacity), "dp", split_axis=0, concat_axis=0, tiled=True
    )
    head_terms = pick_slots(returned.reshape(1, peers * capacity), column)
    return lax.psum(head_terms, "tensor")


def solution(mesh):
    return jax.shard_map(
        on_device,
        mesh=mesh,
        in_specs=(
            P(("groups", "dp"), "tensor"),
            P(("groups", "dp"), None),
            P("groups"),
            P(("groups", "dp"), "tensor"),
            P(("groups", "dp"), "tensor"),
            P("tensor"),
        ),
        out_specs=P(("groups", "dp")),
        check_vma=False,
    )
```

```python
import functools
import math

import jax
import jax.numpy as jnp
from jax import lax
from jax.experimental import pallas as pl
from jax.experimental.pallas import tpu as pltpu
from jax.sharding import PartitionSpec as P

HD = 128
SCALE = math.log2(math.e) / math.sqrt(HD)
MAX_PAIRWISE = 16
QUERY_PARTS = 1


def place_rows(slot_of_token, first_slot, query_ref, out_refs, waits=()):
    slots = sum(out_ref.shape[0] for out_ref in out_refs)
    tok_rows, width = query_ref.shape
    slot_row = first_slot + lax.broadcasted_iota(jnp.int32, (slots, tok_rows), 0)
    picks = (slot_of_token == slot_row).astype(jnp.bfloat16)
    step = width // QUERY_PARTS
    for part in range(QUERY_PARTS):
        columns = slice(part * step, (part + 1) * step)
        if waits:
            waits[part].wait()
        placed = jnp.dot(picks, query_ref[:, columns], preferred_element_type=jnp.float32)
        placed = placed.astype(jnp.bfloat16)
        start = 0
        for out_ref in out_refs:
            out_ref[:, columns] = placed[start : start + out_ref.shape[0]]
            start += out_ref.shape[0]


def route_kernel(peers, capacity, order, owner_hbm, prompt_hbm, query_hbm, column_ref, query_ref, *refs):
    *out_refs, owner_ref, prompt_ref, small_sems, query_sems = refs
    tok_rows, width = query_hbm.shape
    step = width // QUERY_PARTS
    small = [
        pltpu.make_async_copy(owner_hbm, owner_ref, small_sems.at[0]),
        pltpu.make_async_copy(prompt_hbm, prompt_ref, small_sems.at[1]),
    ]
    parts = [
        pltpu.make_async_copy(
            query_hbm.at[:, pl.ds(part * step, step)],
            query_ref.at[:, pl.ds(part * step, step)],
            query_sems.at[part],
        )
        for part in range(QUERY_PARTS)
    ]
    for copy in small + parts:
        copy.start()
    for copy in small:
        copy.wait()
    prompt = prompt_ref[...]
    target = lax.fori_loop(
        0,
        owner_ref.shape[0],
        lambda k, t: jnp.where(prompt == k, owner_ref[k], t),
        jnp.zeros_like(prompt),
        unroll=owner_ref.shape[0] <= MAX_PAIRWISE,
    )
    peer_row = lax.broadcasted_iota(jnp.int32, (peers, tok_rows), 0)
    hits = (target == peer_row).astype(jnp.float32)
    earlier_mask = lax.broadcasted_iota(jnp.int32, (tok_rows, tok_rows), 0) < (
        lax.broadcasted_iota(jnp.int32, (tok_rows, tok_rows), 1)
    )
    earlier = jnp.dot(
        hits.astype(jnp.bfloat16),
        earlier_mask.astype(jnp.bfloat16),
        preferred_element_type=jnp.float32,
    )
    rank = jnp.sum(earlier * hits, axis=0, keepdims=True).astype(jnp.int32)
    place = target
    if order is not None:
        step = target ^ lax.axis_index("dp")
        for position, s in enumerate(order):
            place = jnp.where(step == s, position, place)
    column = place * capacity + rank
    column_ref[...] = column
    place_rows(column, 0, query_ref, out_refs, parts)


def route(queries, answer_prompt, prompt_owner, peers, capacity, order, pieces):
    tok_rows, width = queries.shape
    piece_rows = capacity if order is not None else peers * capacity
    return pl.pallas_call(
        functools.partial(route_kernel, peers, capacity, order),
        in_specs=[pl.BlockSpec(memory_space=pltpu.HBM)] * 3,
        out_specs=[pl.BlockSpec(memory_space=pltpu.VMEM)] * (2 + pieces),
        out_shape=[
            jax.ShapeDtypeStruct((1, tok_rows), jnp.int32),
            jax.ShapeDtypeStruct((tok_rows, width), jnp.bfloat16),
        ]
        + [jax.ShapeDtypeStruct((piece_rows, width), jnp.bfloat16)] * pieces,
        scratch_shapes=[
            pltpu.SMEM(prompt_owner.shape, jnp.int32),
            pltpu.VMEM((1, tok_rows), jnp.int32),
            pltpu.SemaphoreType.DMA((2,)),
            pltpu.SemaphoreType.DMA((QUERY_PARTS,)),
        ],
        compiler_params=pltpu.CompilerParams(vmem_limit_bytes=24 << 20),
        name="route",
    )(
        pltpu.with_memory_space_constraint(prompt_owner, pltpu.HBM),
        pltpu.with_memory_space_constraint(answer_prompt.reshape(1, tok_rows), pltpu.HBM),
        pltpu.with_memory_space_constraint(queries, pltpu.HBM),
    )


def route_rest_kernel(first_slot, column_ref, query_ref, *out_refs):
    place_rows(column_ref[...], first_slot, query_ref, out_refs)


def route_rest(queries, column, first_piece, pieces, capacity):
    return pl.pallas_call(
        functools.partial(route_rest_kernel, first_piece * capacity),
        in_specs=[pl.BlockSpec(memory_space=pltpu.VMEM)] * 2,
        out_specs=[pl.BlockSpec(memory_space=pltpu.VMEM)] * pieces,
        out_shape=[jax.ShapeDtypeStruct((capacity, queries.shape[1]), jnp.bfloat16)] * pieces,
        compiler_params=pltpu.CompilerParams(vmem_limit_bytes=24 << 20),
        name="route_rest",
    )(column, queries)


def attend_block(query_ref, key_ref, value_ref, weight_ref, shift_by_peak):
    rows = query_ref.shape[0]
    kv_local = key_ref.shape[1] // HD
    group_size = query_ref.shape[1] // key_ref.shape[1]
    total = jnp.zeros((rows, HD), jnp.float32)
    smallest = largest = None
    for g in range(kv_local):
        heads = [slice((g * group_size + h) * HD, (g * group_size + h + 1) * HD) for h in range(group_size)]
        kv = slice(g * HD, (g + 1) * HD)
        stacked = jnp.concatenate([query_ref[:, head] for head in heads], axis=0)
        logits = lax.dot_general(
            stacked, key_ref[:, kv], (((1,), (1,)), ((), ())), preferred_element_type=jnp.float32
        )
        if shift_by_peak:
            logits = logits - jnp.max(logits, axis=1, keepdims=True)
        exponent = jnp.exp2(logits * SCALE)
        norm = jnp.sum(exponent, axis=1, keepdims=True)
        smallest = norm if g == 0 else jnp.minimum(smallest, norm)
        largest = norm if g == 0 else jnp.maximum(largest, norm)
        probs = (exponent * (1.0 / norm)).astype(jnp.bfloat16)
        attended = jnp.dot(probs, value_ref[:, kv], preferred_element_type=jnp.float32)
        attended = attended.astype(jnp.bfloat16).astype(jnp.float32)
        for h, head in enumerate(heads):
            total += attended[h * rows : (h + 1) * rows] * weight_ref[:, head]
    return jnp.sum(total.T, axis=0, keepdims=True), jnp.min(smallest), jnp.max(largest)


def attend_kernel(query_ref, key_ref, value_ref, weight_ref, score_ref):
    score, smallest, largest = attend_block(query_ref, key_ref, value_ref, weight_ref, False)
    score_ref[0] = score

    @pl.when(jnp.logical_not((smallest > 1e-25) & (largest < 1e25)))
    def _():
        score_ref[0] = attend_block(query_ref, key_ref, value_ref, weight_ref, True)[0]


def attend_score(query_rows, key_rows, value_rows, score_weight):
    row_count, width = query_rows.shape
    context_len, kv_width = key_rows.shape
    block = math.gcd(row_count, 32)
    blocks = row_count // block
    return pl.pallas_call(
        attend_kernel,
        grid=(blocks,),
        in_specs=[pl.BlockSpec((block, width), lambda r: (r, 0))]
        + [pl.BlockSpec(memory_space=pltpu.VMEM)] * 3,
        out_specs=pl.BlockSpec((1, 1, block), lambda r: (r, 0, 0)),
        out_shape=jax.ShapeDtypeStruct((blocks, 1, block), jnp.float32),
        compiler_params=pltpu.CompilerParams(vmem_limit_bytes=24 << 20),
        cost_estimate=pl.CostEstimate(flops=1 << 20, bytes_accessed=1 << 10, transcendentals=0),
        name="attend_score",
    )(query_rows, key_rows, value_rows, score_weight.reshape(1, -1)).reshape(1, row_count)


def pick_slots(returned, column):
    slots = lax.broadcasted_iota(jnp.int32, (column.shape[1], returned.shape[1]), 1)
    return jnp.sum(jnp.where(column.reshape(-1, 1) == slots, returned, 0.0), axis=1)


def send_order(peers):
    if peers == 8:
        return (7, 1, 2, 3, 5, 6, 4, 0)
    return tuple(range(1, peers)) + (0,)


def on_device(queries, answer_prompt, prompt_owner, context_keys, context_values, score_weight):
    tok_rows, width = queries.shape
    peers = lax.axis_size("dp")
    cores = lax.axis_size("tensor")
    capacity = max(2, 2 * tok_rows // peers)
    by_xor = peers <= MAX_PAIRWISE and peers & (peers - 1) == 0 and capacity % 16 == 0
    order = send_order(peers) if by_xor else None
    early = 3 if by_xor else 1
    column, held_queries, *pieces = route(
        queries, answer_prompt, prompt_owner, peers, capacity, order, early
    )
    context_keys, context_values, score_weight, column = lax.optimization_barrier(
        (context_keys, context_values, score_weight, column)
    )
    score = functools.partial(
        attend_score,
        key_rows=context_keys,
        value_rows=context_values,
        score_weight=score_weight,
    )
    if by_xor:
        pairs = [[(k, k ^ s) for k in range(peers)] for s in range(peers)]
        pieces += route_rest(held_queries, column, early, peers - early, capacity)
        arrived = [
            lax.ppermute(piece, "dp", pairs[s]) if s else piece for s, piece in zip(order, pieces)
        ]
        held = {s: [] for s in range(peers)}
        bits = [1 << b for b in range(peers.bit_length() - 1)]

        def hand_on(bit):
            ways = [s for s in range(bit, peers, 2 * bit)]
            steps = [step for way in ways for step, _ in held[way]]
            scores = jnp.concatenate([part for way in ways for _, part in held[way]], axis=1)
            parts = jnp.split(lax.ppermute(scores, "dp", pairs[bit]), len(steps), axis=1)
            for way in ways:
                for _ in held.pop(way):
                    held[way ^ bit].append((steps.pop(0), parts.pop(0)))

        def after(rows, bit):
            step, part = held[0][-1]
            rows, part = lax.optimization_barrier((rows, part))
            held[0][-1] = step, part
            return rows

        turns = [k for k in range(peers) if order[k]]
        turns.insert(1, order.index(0))
        last = None
        for turn, k in enumerate(turns):
            rows = arrived[k]
            if last is not None:
                rows, last = lax.optimization_barrier((rows, last))
            if turn == 6:
                hand_on(1)
            if turn == 7:
                rows = after(rows, 1)
            if turn == 7:
                hand_on(2)
            last = score(rows)
            held[order[k]].append((order[k], last))
        ways = [0, bits[-1]]
        mine = {way: jnp.concatenate([part for _, part in held[way]], axis=1) for way in ways}
        sums = []
        for way in ways:
            total = mine[way] if way == 0 else lax.ppermute(mine[way], "dp", pairs[way])
            for shift in range(1, cores):
                total += lax.ppermute(
                    mine[way],
                    ("dp", "tensor"),
                    [
                        (k * cores + c, (k ^ way) * cores + (c + shift) % cores)
                        for k in range(peers)
                        for c in range(cores)
                    ],
                )
            sums.append(total)
        back = jnp.zeros_like(column)
        steps = [step for way in ways for step, _ in held[way]]
        for position, step in enumerate(order):
            back = jnp.where(column // capacity == position, steps.index(step), back)
        back = back * capacity + column % capacity
        return pick_slots(jnp.concatenate(sums, axis=1), back)
    arrived = lax.all_to_all(
        pieces[0].reshape(peers, capacity, width), "dp", split_axis=0, concat_axis=0, tiled=True
    )
    own = score(arrived.reshape(peers * capacity, width))
    returned = lax.all_to_all(
        own.reshape(peers, capacity), "dp", split_axis=0, concat_axis=0, tiled=True
    )
    head_terms = pick_slots(returned.reshape(1, peers * capacity), column)
    return lax.psum(head_terms, "tensor")


def solution(mesh):
    return jax.shard_map(
        on_device,
        mesh=mesh,
        in_specs=(
            P(("groups", "dp"), "tensor"),
            P(("groups", "dp"), None),
            P("groups"),
            P(("groups", "dp"), "tensor"),
            P(("groups", "dp"), "tensor"),
            P("tensor"),
        ),
        out_specs=P(("groups", "dp")),
        check_vma=False,
    )
```

```python
import functools
import math

import jax
import jax.numpy as jnp
from jax import lax
from jax.experimental import pallas as pl
from jax.experimental.pallas import tpu as pltpu
from jax.sharding import PartitionSpec as P

HD = 128
SCALE = math.log2(math.e) / math.sqrt(HD)
PAIRWISE = 8
QUERY_PARTS = 1
SEND_ORDER = (7, 2, 1, 3, 5, 6, 4, 0)


def place_rows(slot_of_token, first_slot, query_ref, out_refs, waits=()):
    slots = sum(out_ref.shape[0] for out_ref in out_refs)
    tok_rows, width = query_ref.shape
    slot_row = first_slot + lax.broadcasted_iota(jnp.int32, (slots, tok_rows), 0)
    picks = (slot_of_token == slot_row).astype(jnp.bfloat16)
    step = width // QUERY_PARTS
    for part in range(QUERY_PARTS):
        columns = slice(part * step, (part + 1) * step)
        if waits:
            waits[part].wait()
        placed = jnp.dot(picks, query_ref[:, columns], preferred_element_type=jnp.float32)
        placed = placed.astype(jnp.bfloat16)
        start = 0
        for out_ref in out_refs:
            out_ref[:, columns] = placed[start : start + out_ref.shape[0]]
            start += out_ref.shape[0]


def route_kernel(peers, capacity, order, owner_hbm, prompt_hbm, query_hbm, column_ref, query_ref, *refs):
    *out_refs, owner_ref, prompt_ref, small_sems, query_sems = refs
    tok_rows, width = query_hbm.shape
    step = width // QUERY_PARTS
    small = [
        pltpu.make_async_copy(owner_hbm, owner_ref, small_sems.at[0]),
        pltpu.make_async_copy(prompt_hbm, prompt_ref, small_sems.at[1]),
    ]
    parts = [
        pltpu.make_async_copy(
            query_hbm.at[:, pl.ds(part * step, step)],
            query_ref.at[:, pl.ds(part * step, step)],
            query_sems.at[part],
        )
        for part in range(QUERY_PARTS)
    ]
    for copy in small + parts:
        copy.start()
    for copy in small:
        copy.wait()
    prompt = prompt_ref[...]
    target = lax.fori_loop(
        0,
        owner_ref.shape[0],
        lambda k, t: jnp.where(prompt == k, owner_ref[k], t),
        jnp.zeros_like(prompt),
        unroll=owner_ref.shape[0] <= PAIRWISE,
    )
    peer_row = lax.broadcasted_iota(jnp.int32, (peers, tok_rows), 0)
    hits = (target == peer_row).astype(jnp.float32)
    earlier_mask = lax.broadcasted_iota(jnp.int32, (tok_rows, tok_rows), 0) < (
        lax.broadcasted_iota(jnp.int32, (tok_rows, tok_rows), 1)
    )
    earlier = jnp.dot(
        hits.astype(jnp.bfloat16),
        earlier_mask.astype(jnp.bfloat16),
        preferred_element_type=jnp.float32,
    )
    rank = jnp.sum(earlier * hits, axis=0, keepdims=True).astype(jnp.int32)
    place = target
    if order is not None:
        step = target ^ lax.axis_index("dp")
        for position, s in enumerate(order):
            place = jnp.where(step == s, position, place)
    column = place * capacity + rank
    column_ref[...] = column
    place_rows(column, 0, query_ref, out_refs, parts)


def route(queries, answer_prompt, prompt_owner, peers, capacity, order, pieces):
    tok_rows, width = queries.shape
    piece_rows = capacity if order is not None else peers * capacity
    return pl.pallas_call(
        functools.partial(route_kernel, peers, capacity, order),
        in_specs=[pl.BlockSpec(memory_space=pltpu.HBM)] * 3,
        out_specs=[pl.BlockSpec(memory_space=pltpu.VMEM)] * (2 + pieces),
        out_shape=[
            jax.ShapeDtypeStruct((1, tok_rows), jnp.int32),
            jax.ShapeDtypeStruct((tok_rows, width), jnp.bfloat16),
        ]
        + [jax.ShapeDtypeStruct((piece_rows, width), jnp.bfloat16)] * pieces,
        scratch_shapes=[
            pltpu.SMEM(prompt_owner.shape, jnp.int32),
            pltpu.VMEM((1, tok_rows), jnp.int32),
            pltpu.SemaphoreType.DMA((2,)),
            pltpu.SemaphoreType.DMA((QUERY_PARTS,)),
        ],
        compiler_params=pltpu.CompilerParams(vmem_limit_bytes=24 << 20),
        name="route",
    )(
        pltpu.with_memory_space_constraint(prompt_owner, pltpu.HBM),
        pltpu.with_memory_space_constraint(answer_prompt.reshape(1, tok_rows), pltpu.HBM),
        pltpu.with_memory_space_constraint(queries, pltpu.HBM),
    )


def route_rest_kernel(first_slot, column_ref, query_ref, *out_refs):
    place_rows(column_ref[...], first_slot, query_ref, out_refs)


def route_rest(queries, column, first_piece, pieces, capacity):
    return pl.pallas_call(
        functools.partial(route_rest_kernel, first_piece * capacity),
        in_specs=[pl.BlockSpec(memory_space=pltpu.VMEM)] * 2,
        out_specs=[pl.BlockSpec(memory_space=pltpu.VMEM)] * pieces,
        out_shape=[jax.ShapeDtypeStruct((capacity, queries.shape[1]), jnp.bfloat16)] * pieces,
        compiler_params=pltpu.CompilerParams(vmem_limit_bytes=24 << 20),
        name="route_rest",
    )(column, queries)


def attend_block(query_ref, key_ref, value_ref, weight_ref, shift_by_peak):
    rows = query_ref.shape[0]
    kv_local = key_ref.shape[1] // HD
    group_size = query_ref.shape[1] // key_ref.shape[1]
    total = jnp.zeros((rows, HD), jnp.float32)
    smallest = largest = None
    for g in range(kv_local):
        heads = [slice((g * group_size + h) * HD, (g * group_size + h + 1) * HD) for h in range(group_size)]
        kv = slice(g * HD, (g + 1) * HD)
        stacked = jnp.concatenate([query_ref[:, head] for head in heads], axis=0)
        logits = lax.dot_general(
            stacked, key_ref[:, kv], (((1,), (1,)), ((), ())), preferred_element_type=jnp.float32
        )
        if shift_by_peak:
            logits = logits - jnp.max(logits, axis=1, keepdims=True)
        exponent = jnp.exp2(logits * SCALE)
        norm = jnp.sum(exponent, axis=1, keepdims=True)
        smallest = norm if g == 0 else jnp.minimum(smallest, norm)
        largest = norm if g == 0 else jnp.maximum(largest, norm)
        probs = (exponent * (1.0 / norm)).astype(jnp.bfloat16)
        attended = jnp.dot(probs, value_ref[:, kv], preferred_element_type=jnp.float32)
        attended = attended.astype(jnp.bfloat16).astype(jnp.float32)
        for h, head in enumerate(heads):
            total += attended[h * rows : (h + 1) * rows] * weight_ref[:, head]
    return jnp.sum(total.T, axis=0, keepdims=True), jnp.min(smallest), jnp.max(largest)


def attend_kernel(query_ref, key_ref, value_ref, weight_ref, score_ref):
    score, smallest, largest = attend_block(query_ref, key_ref, value_ref, weight_ref, False)
    score_ref[0] = score

    @pl.when(jnp.logical_not((smallest > 1e-25) & (largest < 1e25)))
    def _():
        score_ref[0] = attend_block(query_ref, key_ref, value_ref, weight_ref, True)[0]


def attend_score(query_rows, key_rows, value_rows, score_weight):
    row_count, width = query_rows.shape
    context_len, kv_width = key_rows.shape
    block = math.gcd(row_count, 32)
    blocks = row_count // block
    return pl.pallas_call(
        attend_kernel,
        grid=(blocks,),
        in_specs=[pl.BlockSpec((block, width), lambda r: (r, 0))]
        + [pl.BlockSpec(memory_space=pltpu.VMEM)] * 3,
        out_specs=pl.BlockSpec((1, 1, block), lambda r: (r, 0, 0)),
        out_shape=jax.ShapeDtypeStruct((blocks, 1, block), jnp.float32),
        compiler_params=pltpu.CompilerParams(vmem_limit_bytes=24 << 20),
        cost_estimate=pl.CostEstimate(flops=1 << 20, bytes_accessed=1 << 10, transcendentals=0),
        name="attend_score",
    )(query_rows, key_rows, value_rows, score_weight.reshape(1, -1)).reshape(1, row_count)


def pick_slots(returned, column):
    slots = lax.broadcasted_iota(jnp.int32, (column.shape[1], returned.shape[1]), 1)
    return jnp.sum(jnp.where(column.reshape(-1, 1) == slots, returned, 0.0), axis=1)


def on_device(queries, answer_prompt, prompt_owner, context_keys, context_values, score_weight):
    tok_rows, width = queries.shape
    peers = lax.axis_size("dp")
    cores = lax.axis_size("tensor")
    capacity = max(2, 2 * tok_rows // peers)
    by_xor = peers == PAIRWISE and capacity % 16 == 0
    order = SEND_ORDER if by_xor else None
    early = 3 if by_xor else 1
    column, held_queries, *pieces = route(
        queries, answer_prompt, prompt_owner, peers, capacity, order, early
    )
    context_keys, context_values, score_weight, column = lax.optimization_barrier(
        (context_keys, context_values, score_weight, column)
    )
    score = functools.partial(
        attend_score,
        key_rows=context_keys,
        value_rows=context_values,
        score_weight=score_weight,
    )
    if by_xor:
        pairs = [[(k, k ^ s) for k in range(peers)] for s in range(peers)]
        pieces += route_rest(held_queries, column, early, peers - early, capacity)
        arrived = [
            lax.ppermute(piece, "dp", pairs[s]) if s else piece for s, piece in zip(order, pieces)
        ]
        held = {s: [] for s in range(peers)}
        bits = [1 << b for b in range(peers.bit_length() - 1)]

        def hand_on(bit):
            ways = [s for s in range(bit, peers, 2 * bit)]
            steps = [step for way in ways for step, _ in held[way]]
            scores = jnp.concatenate([part for way in ways for _, part in held[way]], axis=1)
            parts = jnp.split(lax.ppermute(scores, "dp", pairs[bit]), len(steps), axis=1)
            for way in ways:
                for _ in held.pop(way):
                    held[way ^ bit].append((steps.pop(0), parts.pop(0)))

        def after(rows, bit):
            step, part = held[0][-1]
            rows, part = lax.optimization_barrier((rows, part))
            held[0][-1] = step, part
            return rows

        turns = [k for k in range(peers) if order[k]]
        turns.insert(1, order.index(0))
        last = None
        for turn, k in enumerate(turns):
            rows = arrived[k]
            if last is not None:
                rows, last = lax.optimization_barrier((rows, last))
            if turn == 6:
                hand_on(1)
            if turn == 7:
                rows = after(rows, 1)
            if turn == 7:
                hand_on(2)
            last = score(rows)
            held[order[k]].append((order[k], last))
        ways = [0, bits[-1]]
        mine = {way: jnp.concatenate([part for _, part in held[way]], axis=1) for way in ways}
        sums = []
        for way in ways:
            total = mine[way] if way == 0 else lax.ppermute(mine[way], "dp", pairs[way])
            for shift in range(1, cores):
                total += lax.ppermute(
                    mine[way],
                    ("dp", "tensor"),
                    [
                        (k * cores + c, (k ^ way) * cores + (c + shift) % cores)
                        for k in range(peers)
                        for c in range(cores)
                    ],
                )
            sums.append(total)
        back = jnp.zeros_like(column)
        steps = [step for way in ways for step, _ in held[way]]
        for position, step in enumerate(order):
            back = jnp.where(column // capacity == position, steps.index(step), back)
        back = back * capacity + column % capacity
        return pick_slots(jnp.concatenate(sums, axis=1), back)
    arrived = lax.all_to_all(
        pieces[0].reshape(peers, capacity, width), "dp", split_axis=0, concat_axis=0, tiled=True
    )
    own = score(arrived.reshape(peers * capacity, width))
    returned = lax.all_to_all(
        own.reshape(peers, capacity), "dp", split_axis=0, concat_axis=0, tiled=True
    )
    head_terms = pick_slots(returned.reshape(1, peers * capacity), column)
    return lax.psum(head_terms, "tensor")


def solution(mesh):
    return jax.shard_map(
        on_device,
        mesh=mesh,
        in_specs=(
            P(("groups", "dp"), "tensor"),
            P(("groups", "dp"), None),
            P("groups"),
            P(("groups", "dp"), "tensor"),
            P(("groups", "dp"), "tensor"),
            P("tensor"),
        ),
        out_specs=P(("groups", "dp")),
        check_vma=False,
    )
```

```python
import functools
import math

import jax
import jax.numpy as jnp
from jax import lax
from jax.experimental import pallas as pl
from jax.experimental.pallas import tpu as pltpu
from jax.sharding import PartitionSpec as P

HD = 128
SCALE = math.log2(math.e) / math.sqrt(HD)
PAIRWISE = 8
QUERY_PARTS = 1
SEND_ORDER = (7, 2, 1, 3, 6, 5, 4, 0)


def place_rows(slot_of_token, first_slot, query_ref, out_refs, waits=()):
    slots = sum(out_ref.shape[0] for out_ref in out_refs)
    tok_rows, width = query_ref.shape
    slot_row = first_slot + lax.broadcasted_iota(jnp.int32, (slots, tok_rows), 0)
    picks = (slot_of_token == slot_row).astype(jnp.bfloat16)
    step = width // QUERY_PARTS
    for part in range(QUERY_PARTS):
        columns = slice(part * step, (part + 1) * step)
        if waits:
            waits[part].wait()
        placed = jnp.dot(picks, query_ref[:, columns], preferred_element_type=jnp.float32)
        placed = placed.astype(jnp.bfloat16)
        start = 0
        for out_ref in out_refs:
            out_ref[:, columns] = placed[start : start + out_ref.shape[0]]
            start += out_ref.shape[0]


def route_kernel(peers, capacity, order, owner_hbm, prompt_hbm, query_hbm, column_ref, query_ref, *refs):
    *out_refs, owner_ref, prompt_ref, small_sems, query_sems = refs
    tok_rows, width = query_hbm.shape
    step = width // QUERY_PARTS
    small = [
        pltpu.make_async_copy(owner_hbm, owner_ref, small_sems.at[0]),
        pltpu.make_async_copy(prompt_hbm, prompt_ref, small_sems.at[1]),
    ]
    parts = [
        pltpu.make_async_copy(
            query_hbm.at[:, pl.ds(part * step, step)],
            query_ref.at[:, pl.ds(part * step, step)],
            query_sems.at[part],
        )
        for part in range(QUERY_PARTS)
    ]
    for copy in small + parts:
        copy.start()
    for copy in small:
        copy.wait()
    prompt = prompt_ref[...]
    target = lax.fori_loop(
        0,
        owner_ref.shape[0],
        lambda k, t: jnp.where(prompt == k, owner_ref[k], t),
        jnp.zeros_like(prompt),
        unroll=owner_ref.shape[0] <= PAIRWISE,
    )
    peer_row = lax.broadcasted_iota(jnp.int32, (peers, tok_rows), 0)
    hits = (target == peer_row).astype(jnp.float32)
    earlier_mask = lax.broadcasted_iota(jnp.int32, (tok_rows, tok_rows), 0) < (
        lax.broadcasted_iota(jnp.int32, (tok_rows, tok_rows), 1)
    )
    earlier = jnp.dot(
        hits.astype(jnp.bfloat16),
        earlier_mask.astype(jnp.bfloat16),
        preferred_element_type=jnp.float32,
    )
    rank = jnp.sum(earlier * hits, axis=0, keepdims=True).astype(jnp.int32)
    place = target
    if order is not None:
        step = target ^ lax.axis_index("dp")
        for position, s in enumerate(order):
            place = jnp.where(step == s, position, place)
    column = place * capacity + rank
    column_ref[...] = column
    place_rows(column, 0, query_ref, out_refs, parts)


def route(queries, answer_prompt, prompt_owner, peers, capacity, order, pieces):
    tok_rows, width = queries.shape
    piece_rows = capacity if order is not None else peers * capacity
    return pl.pallas_call(
        functools.partial(route_kernel, peers, capacity, order),
        in_specs=[pl.BlockSpec(memory_space=pltpu.HBM)] * 3,
        out_specs=[pl.BlockSpec(memory_space=pltpu.VMEM)] * (2 + pieces),
        out_shape=[
            jax.ShapeDtypeStruct((1, tok_rows), jnp.int32),
            jax.ShapeDtypeStruct((tok_rows, width), jnp.bfloat16),
        ]
        + [jax.ShapeDtypeStruct((piece_rows, width), jnp.bfloat16)] * pieces,
        scratch_shapes=[
            pltpu.SMEM(prompt_owner.shape, jnp.int32),
            pltpu.VMEM((1, tok_rows), jnp.int32),
            pltpu.SemaphoreType.DMA((2,)),
            pltpu.SemaphoreType.DMA((QUERY_PARTS,)),
        ],
        compiler_params=pltpu.CompilerParams(vmem_limit_bytes=24 << 20),
        name="route",
    )(
        pltpu.with_memory_space_constraint(prompt_owner, pltpu.HBM),
        pltpu.with_memory_space_constraint(answer_prompt.reshape(1, tok_rows), pltpu.HBM),
        pltpu.with_memory_space_constraint(queries, pltpu.HBM),
    )


def route_rest_kernel(first_slot, column_ref, query_ref, *out_refs):
    place_rows(column_ref[...], first_slot, query_ref, out_refs)


def route_rest(queries, column, first_piece, pieces, capacity):
    return pl.pallas_call(
        functools.partial(route_rest_kernel, first_piece * capacity),
        in_specs=[pl.BlockSpec(memory_space=pltpu.VMEM)] * 2,
        out_specs=[pl.BlockSpec(memory_space=pltpu.VMEM)] * pieces,
        out_shape=[jax.ShapeDtypeStruct((capacity, queries.shape[1]), jnp.bfloat16)] * pieces,
        compiler_params=pltpu.CompilerParams(vmem_limit_bytes=24 << 20),
        name="route_rest",
    )(column, queries)


def attend_block(query_ref, key_ref, value_ref, weight_ref, shift_by_peak):
    rows = query_ref.shape[0]
    kv_local = key_ref.shape[1] // HD
    group_size = query_ref.shape[1] // key_ref.shape[1]
    total = jnp.zeros((rows, HD), jnp.float32)
    smallest = largest = None
    for g in range(kv_local):
        heads = [slice((g * group_size + h) * HD, (g * group_size + h + 1) * HD) for h in range(group_size)]
        kv = slice(g * HD, (g + 1) * HD)
        stacked = jnp.concatenate([query_ref[:, head] for head in heads], axis=0)
        logits = lax.dot_general(
            stacked, key_ref[:, kv], (((1,), (1,)), ((), ())), preferred_element_type=jnp.float32
        )
        if shift_by_peak:
            logits = logits - jnp.max(logits, axis=1, keepdims=True)
        exponent = jnp.exp2(logits * SCALE)
        norm = jnp.sum(exponent, axis=1, keepdims=True)
        smallest = norm if g == 0 else jnp.minimum(smallest, norm)
        largest = norm if g == 0 else jnp.maximum(largest, norm)
        probs = (exponent * (1.0 / norm)).astype(jnp.bfloat16)
        attended = jnp.dot(probs, value_ref[:, kv], preferred_element_type=jnp.float32)
        attended = attended.astype(jnp.bfloat16).astype(jnp.float32)
        for h, head in enumerate(heads):
            total += attended[h * rows : (h + 1) * rows] * weight_ref[:, head]
    return jnp.sum(total.T, axis=0, keepdims=True), jnp.min(smallest), jnp.max(largest)


def attend_kernel(query_ref, key_ref, value_ref, weight_ref, score_ref):
    score, smallest, largest = attend_block(query_ref, key_ref, value_ref, weight_ref, False)
    score_ref[0] = score

    @pl.when(jnp.logical_not((smallest > 1e-25) & (largest < 1e25)))
    def _():
        score_ref[0] = attend_block(query_ref, key_ref, value_ref, weight_ref, True)[0]


def attend_score(query_rows, key_rows, value_rows, score_weight):
    row_count, width = query_rows.shape
    context_len, kv_width = key_rows.shape
    block = math.gcd(row_count, 32)
    blocks = row_count // block
    return pl.pallas_call(
        attend_kernel,
        grid=(blocks,),
        in_specs=[pl.BlockSpec((block, width), lambda r: (r, 0))]
        + [pl.BlockSpec(memory_space=pltpu.VMEM)] * 3,
        out_specs=pl.BlockSpec((1, 1, block), lambda r: (r, 0, 0)),
        out_shape=jax.ShapeDtypeStruct((blocks, 1, block), jnp.float32),
        compiler_params=pltpu.CompilerParams(vmem_limit_bytes=24 << 20),
        cost_estimate=pl.CostEstimate(flops=1 << 20, bytes_accessed=1 << 10, transcendentals=0),
        name="attend_score",
    )(query_rows, key_rows, value_rows, score_weight.reshape(1, -1)).reshape(1, row_count)


def pick_slots(returned, column):
    slots = lax.broadcasted_iota(jnp.int32, (column.shape[1], returned.shape[1]), 1)
    return jnp.sum(jnp.where(column.reshape(-1, 1) == slots, returned, 0.0), axis=1)


def on_device(queries, answer_prompt, prompt_owner, context_keys, context_values, score_weight):
    tok_rows, width = queries.shape
    peers = lax.axis_size("dp")
    cores = lax.axis_size("tensor")
    capacity = max(2, 2 * tok_rows // peers)
    by_xor = peers == PAIRWISE and capacity % 16 == 0
    order = SEND_ORDER if by_xor else None
    early = 3 if by_xor else 1
    column, held_queries, *pieces = route(
        queries, answer_prompt, prompt_owner, peers, capacity, order, early
    )
    context_keys, context_values, score_weight, column = lax.optimization_barrier(
        (context_keys, context_values, score_weight, column)
    )
    score = functools.partial(
        attend_score,
        key_rows=context_keys,
        value_rows=context_values,
        score_weight=score_weight,
    )
    if by_xor:
        pairs = [[(k, k ^ s) for k in range(peers)] for s in range(peers)]
        pieces += route_rest(held_queries, column, early, peers - early, capacity)
        arrived = [
            lax.ppermute(piece, "dp", pairs[s]) if s else piece for s, piece in zip(order, pieces)
        ]
        held = {s: [] for s in range(peers)}
        bits = [1 << b for b in range(peers.bit_length() - 1)]

        def hand_on(bit):
            ways = [s for s in sorted(held) if s & bit]
            steps = [step for way in ways for step, _ in held[way]]
            scores = jnp.concatenate([part for way in ways for _, part in held[way]], axis=1)
            parts = jnp.split(lax.ppermute(scores, "dp", pairs[bit]), len(steps), axis=1)
            for way in ways:
                for _ in held.pop(way):
                    held[way ^ bit].append((steps.pop(0), parts.pop(0)))

        def after(rows, bit):
            step, part = held[0][-1]
            rows, part = lax.optimization_barrier((rows, part))
            held[0][-1] = step, part
            return rows

        turns = [k for k in range(peers) if order[k]]
        turns.insert(1, order.index(0))
        last = None
        for turn, k in enumerate(turns):
            rows = arrived[k]
            if last is not None:
                rows, last = lax.optimization_barrier((rows, last))
            if turn == 6:
                hand_on(2)
            if turn == 7:
                rows = after(rows, 1)
            if turn == 7:
                hand_on(1)
            last = score(rows)
            held[order[k]].append((order[k], last))
        ways = [0, bits[-1]]
        mine = {way: jnp.concatenate([part for _, part in held[way]], axis=1) for way in ways}
        sums = []
        for way in ways:
            total = mine[way] if way == 0 else lax.ppermute(mine[way], "dp", pairs[way])
            for shift in range(1, cores):
                total += lax.ppermute(
                    mine[way],
                    ("dp", "tensor"),
                    [
                        (k * cores + c, (k ^ way) * cores + (c + shift) % cores)
                        for k in range(peers)
                        for c in range(cores)
                    ],
                )
            sums.append(total)
        back = jnp.zeros_like(column)
        steps = [step for way in ways for step, _ in held[way]]
        for position, step in enumerate(order):
            back = jnp.where(column // capacity == position, steps.index(step), back)
        back = back * capacity + column % capacity
        return pick_slots(jnp.concatenate(sums, axis=1), back)
    arrived = lax.all_to_all(
        pieces[0].reshape(peers, capacity, width), "dp", split_axis=0, concat_axis=0, tiled=True
    )
    own = score(arrived.reshape(peers * capacity, width))
    returned = lax.all_to_all(
        own.reshape(peers, capacity), "dp", split_axis=0, concat_axis=0, tiled=True
    )
    head_terms = pick_slots(returned.reshape(1, peers * capacity), column)
    return lax.psum(head_terms, "tensor")


def solution(mesh):
    return jax.shard_map(
        on_device,
        mesh=mesh,
        in_specs=(
            P(("groups", "dp"), "tensor"),
            P(("groups", "dp"), None),
            P("groups"),
            P(("groups", "dp"), "tensor"),
            P(("groups", "dp"), "tensor"),
            P("tensor"),
        ),
        out_specs=P(("groups", "dp")),
        check_vma=False,
    )
```
